32 devices in a mesh: row: 4 (over x, core), col: 8 (over z, y).
Axes of the slice: x: 2, y: 2, z: 4, core: 2. Of those that a mesh axis runs over, the one named last changes fastest.
Arguments:
- source: float32 [32768, 256], P(('row', 'col')), may hold values from -6 to 6
- leaf_in: float32 [128, 128, 256], P(('row', 'col')), may hold values from -0.375 to 0.375
- factors: float32 [7, 128, 128, 256], P(None, ('row', 'col')), may hold values from -0.375 to 0.375
- leaf_out: float32 [128, 256, 128], P(('row', 'col')), may hold values from -0.5 to 0.5
- weight_table: float32 [128, 256], P(('row', 'col')), may hold values from 0.25 to 4
- block_index: int32 [128], P(('row', 'col')), may hold values from 0 to 127
Outputs:
- result: float32 [32768, 256], P(('row', 'col'))
The draws below stay inside these ranges and needn't reach their ends.
All inputs are finite; a program needn't handle non-finite values.
Results may differ from the reference program's by a relative error of at most 0.0001.
Values sent between devices are 32-bit elements; how exact they have to be, the bound alone decides.
No kernel may reach another device: no remote copies, remote signals or barrier semaphores. Data moves between devices by JAX's collectives and lax.ppermute only.
A program may use at most 64 MiB of HBM per device.

```python
import math
import jax
import jax.numpy as jnp
from jax import lax

LEAF = 256
RANK = 128
RHS = 256
LEVELS = 7
NODES = 128


def set_ends(entries, stream_key, smallest, top_value):
    longest = entries.shape.index(max(entries.shape))
    spots = []
    for shift in (0, 1):
        where = [jax.random.randint(jax.random.fold_in(stream_key, axis), (), 0, length) for axis, length in enumerate(entries.shape)]
        where[longest] = (where[longest] + shift) % entries.shape[longest]
        spots.append(tuple(where))
    return entries.at[spots[0]].set(smallest).at[spots[1]].set(top_value)


def block_levels(own_key, dims, split, low, top_value):
    level, own = 1.0, jax.random.fold_in(own_key, 6)
    for axis_at, shards_of in split:
        heights = jnp.exp(jax.random.uniform(jax.random.fold_in(own, axis_at), (shards_of,), jnp.float32, low / len(split), top_value / len(split)))
        level = level * jnp.repeat(heights, dims[axis_at] // shards_of).reshape([-1 if axis == axis_at else 1 for axis in range(len(dims))])
    return level


def normal_values(key, extent, spread, reach, pieces=(), held_as=jnp.bfloat16):
    values = jax.random.normal(key, extent, jnp.float32) * spread
    if len(pieces) > 0:
        values = block_levels(key, extent, pieces, -0.22, 0.18) * values
    return jnp.clip(values, min=-reach, max=reach).astype(held_as)


def setup_inputs(seed: int = 0) -> dict:
    splits = jax.random.split(jax.random.key(seed), 7)
    return {
        "source": normal_values(splits[0], (NODES * LEAF, RHS), 1.0, 6.0, ((0, 32),), jnp.float32),
        "leaf_in": normal_values(splits[1], (NODES, RANK, LEAF), LEAF ** -0.5, 0.375, ((0, 32),), jnp.float32),
        "factors": normal_values(splits[2], (LEVELS, NODES, RANK, 2 * RANK), (2 * RANK) ** -0.5, 0.375, ((1, 32),), jnp.float32),
        "leaf_out": normal_values(splits[3], (NODES, LEAF, RANK), RANK ** -0.5, 0.5, ((0, 32),), jnp.float32),
        "weight_table": jnp.clip(jnp.exp(math.log(4.0) - 2.7725887 * jax.random.uniform(splits[4], (NODES, LEAF), jnp.float32) ** block_levels(splits[4], (NODES, LEAF), ((0, 32),), -0.2, 0.2)), 0.25, 4.0),
        "block_index": set_ends(jax.random.randint(splits[5], (NODES,), 0, NODES), jax.random.fold_in(splits[5], 1), 0, NODES - 1).astype(jnp.int32),
    }


HIGH = lax.Precision.HIGHEST


def swap_nodes(blocks, level_index):
    stride = 1 << level_index
    node_count = blocks.shape[0]
    shaped = blocks.reshape(node_count // (2 * stride), 2, stride, blocks.shape[1], blocks.shape[2])
    return shaped[:, ::-1].reshape(blocks.shape)


def reference(source, leaf_in, factors, leaf_out, weight_table, block_index):
    level_count = factors.shape[0]
    leaves = source.reshape(NODES, LEAF, RHS)
    coefficients = jnp.einsum("nrk,nks->nrs", leaf_in, leaves, precision=HIGH)
    for level_index in range(level_count):
        stacked = jnp.concatenate([coefficients, swap_nodes(coefficients, level_index)], axis=1)
        coefficients = jnp.einsum("nrk,nks->nrs", factors[level_index], stacked, precision=HIGH)
    image = jnp.einsum("nlr,nrs->nls", leaf_out, coefficients, precision=HIGH)
    profiles = weight_table[block_index.astype(jnp.int32)]
    scaled = profiles[:, :, None] * image
    adjoint = jnp.einsum("nlr,nls->nrs", leaf_out, scaled, precision=HIGH)
    for level_index in reversed(range(level_count)):
        own_part = factors[level_index][:, :, :RANK]
        cross_part = factors[level_index][:, :, RANK:]
        cross_term = jnp.einsum("nrk,nrs->nks", cross_part, adjoint, precision=HIGH)
        adjoint = jnp.einsum("nrk,nrs->nks", own_part, adjoint, precision=HIGH) + swap_nodes(cross_term, level_index)
    result = jnp.einsum("nrl,nrs->nls", leaf_in, adjoint, precision=HIGH)
    return result.reshape(NODES * LEAF, RHS)
```

```python
import jax
import jax.numpy as jnp
from jax import lax
from jax.sharding import PartitionSpec as P

HIGH = lax.Precision.HIGHEST


def exchange(value, axis, bit):
    return lax.ppermute(value, axis, [(i, i ^ 1 << bit) for i in range(lax.axis_size(axis))])


def gather_rows(weight_table, block_index, steps):
    table = weight_table
    col_size = lax.axis_size("col")
    own = lax.axis_index("row") * col_size + lax.axis_index("col")
    rows_each = weight_table.shape[0]
    differs = (block_index // rows_each) ^ own
    place = jnp.zeros_like(block_index)
    for count, (axis, bit) in enumerate(steps):
        table = jnp.concatenate([table, exchange(table, axis, bit)], axis=0)
        shift = bit if axis == "col" else bit + col_size.bit_length() - 1
        place = place | (((differs >> shift) & 1) << count)
    return table[place * rows_each + block_index % rows_each]


def body(source, leaf_in, factors, leaf_out, weight_table, block_index):
    level_count = factors.shape[0]
    node_count, rank_size, leaf_size = leaf_in.shape
    column_count = source.shape[1]
    local_bits = node_count.bit_length() - 1
    col_bits = lax.axis_size("col").bit_length() - 1
    row_bits = lax.axis_size("row").bit_length() - 1
    where = {}
    for level_index in range(local_bits, level_count):
        position = level_index - local_bits
        where[level_index] = ("col", position) if position < col_bits else ("row", position - col_bits)
    steps = [("col", b) for b in reversed(range(col_bits))] + [("row", b) for b in reversed(range(row_bits))]
    profiles = gather_rows(weight_table, block_index, steps)

    leaves = source.reshape(node_count, leaf_size, column_count)
    coefficients = [jnp.dot(leaf_in[j], leaves[j], precision=HIGH) for j in range(node_count)]
    for level_index in range(local_bits):
        coefficients = [
            jnp.dot(
                factors[level_index, j],
                jnp.concatenate([coefficients[j], coefficients[j ^ 1 << level_index]], axis=0),
                precision=HIGH,
            )
            for j in range(node_count)
        ]

    def remote_part(j, value):
        for level_index in range(local_bits, level_count):
            received = exchange(value, *where[level_index])
            value = jnp.dot(factors[level_index, j], jnp.concatenate([value, received], axis=0), precision=HIGH)
        image = jnp.dot(leaf_out[j], value, precision=HIGH)
        scaled = profiles[j][:, None] * image
        value = jnp.einsum("lr,ls->rs", leaf_out[j], scaled, precision=HIGH)
        for level_index in reversed(range(local_bits, level_count)):
            both = jnp.einsum("rk,rs->ks", factors[level_index, j], value, precision=HIGH)
            value = both[:rank_size] + exchange(both[rank_size:], *where[level_index])
        return value

    adjoint = [remote_part(j, coefficients[j]) for j in range(node_count)]
    for level_index in reversed(range(local_bits)):
        both = [jnp.einsum("rk,rs->ks", factors[level_index, j], adjoint[j], precision=HIGH) for j in range(node_count)]
        adjoint = [both[j][:rank_size] + both[j ^ 1 << level_index][rank_size:] for j in range(node_count)]
    result = [jnp.einsum("rl,rs->ls", leaf_in[j], adjoint[j], precision=HIGH) for j in range(node_count)]
    return jnp.concatenate(result, axis=0)


def solution(mesh):
    placed = (
        P(("row", "col"), None),
        P(("row", "col"), None, None),
        P(None, ("row", "col"), None, None),
        P(("row", "col"), None, None),
        P(("row", "col"), None),
        P(("row", "col")),
    )
    return jax.shard_map(
        body, mesh=mesh, in_specs=placed, out_specs=P(("row", "col"), None), check_vma=False
    )
```

```python
import functools

import jax
import jax.numpy as jnp
from jax import lax
from jax.experimental import pallas as pl
from jax.experimental.pallas import tpu as pltpu
from jax.sharding import PartitionSpec as P

CHUNKS = 2
MIB = 1 << 20
VMEM = pl.BlockSpec(memory_space=pltpu.VMEM)
SMEM = pl.BlockSpec(memory_space=pltpu.SMEM)
HBM = pl.BlockSpec(memory_space=pltpu.HBM)


def exchange(value, axis, bit):
    return lax.ppermute(value, axis, [(i, i ^ 1 << bit) for i in range(lax.axis_size(axis))])


def split(value):
    high = value.astype(jnp.bfloat16)
    return high, (value - high.astype(jnp.float32)).astype(jnp.bfloat16)


def product(a, b):
    one = functools.partial(jnp.dot, preferred_element_type=jnp.float32)
    return one(a[0], b[1]) + one(a[1], b[0]) + one(a[0], b[0])


def turned(value):
    return split(value.T)


def call(kernel, outs, specs, out_specs, flops, traffic, scratch=(), limit=8 * MIB):
    return pl.pallas_call(
        kernel,
        out_shape=outs,
        in_specs=specs,
        out_specs=out_specs,
        scratch_shapes=scratch,
        cost_estimate=pl.CostEstimate(flops=flops, bytes_accessed=traffic, transcendentals=0),
        compiler_params=pltpu.CompilerParams(vmem_limit_bytes=limit),
    )


def start_kernel(nodes, rank, leaf, local_bits, chunks, source, leaf_in, factors, table, *rest):
    outs, (x, a, f, sems) = rest[:chunks], rest[chunks:]
    levels = [pltpu.make_async_copy(factors.at[l], f.at[l], sems.at[2 * nodes + l]) for l in range(local_bits)]
    xs = [pltpu.make_async_copy(source.at[pl.ds(j * leaf, leaf)], x.at[j], sems.at[j]) for j in range(nodes)]
    ins = [pltpu.make_async_copy(leaf_in.at[j], a.at[j], sems.at[nodes + j]) for j in range(nodes)]
    for j in range(nodes):
        ins[j].start()
        xs[j].start()
    for copy in levels:
        copy.start()
    values = []
    for j in range(nodes):
        ins[j].wait()
        xs[j].wait()
        values.append(product(split(a[j]), split(x[j])))
    for l in range(local_bits):
        levels[l].wait()
        halves = [split(v) for v in values]
        values = []
        for j in range(nodes):
            mine, other = halves[j], halves[j ^ 1 << l]
            both = tuple(jnp.concatenate([m, o], axis=0) for m, o in zip(mine, other))
            values.append(product(split(f[l, j]), both))
    per = nodes // chunks
    for j in range(nodes):
        outs[j // per][pl.ds((j % per) * rank, rank), :] = values[j]
    extra = table.shape[0]
    outs[0][pl.ds(per * rank, extra), :] = table[...]


def forward_kernel(first, per, rank, level, own, got, factors, out):
    for i in range(per):
        rows = pl.ds(i * rank, rank)
        both = split(jnp.concatenate([own[rows, :], got[rows, :]], axis=0))
        out[rows, :] = product(split(factors[level, first + i]), both)
    extra = own.shape[0] - per * rank
    if extra:
        tail = pl.ds(per * rank, extra)
        out[tail, :] = own[tail, :]
        out[pl.ds(per * rank + extra, extra), :] = got[tail, :]


def middle_kernel(first, per, rank, level, index, own, got, tab_own, tab_got, factors, leaf_out, keep, send):
    half = tab_own.shape[0] - per * rank
    for i in range(per):
        rows = pl.ds(i * rank, rank)
        f = factors[level, first + i]
        value = product(split(f), split(jnp.concatenate([own[rows, :], got[rows, :]], axis=0)))
        l = leaf_out[first + i]
        image = product(split(l), split(value))
        at = index[first + i]
        near = per * rank + jnp.where(at < half, at, at - half)
        weights = jnp.where(at < half, tab_own[pl.ds(near, 1), :], tab_got[pl.ds(near, 1), :])
        value = product(split(l.T * weights), split(image))
        both = product(turned(f), split(value))
        keep[rows, :] = both[:rank]
        send[rows, :] = both[rank:]


def backward_kernel(first, per, rank, level, own, got, factors, keep, send):
    for i in range(per):
        rows = pl.ds(i * rank, rank)
        both = product(turned(factors[level, first + i]), split(own[rows, :] + got[rows, :]))
        keep[rows, :] = both[:rank]
        send[rows, :] = both[rank:]


def end_kernel(nodes, rank, leaf, local_bits, chunks, leaf_in, factors, *rest):
    pairs, out, (y, sems) = rest[: 2 * chunks], rest[2 * chunks], rest[2 * chunks + 1 :]
    per = nodes // chunks
    values = []
    for j in range(nodes):
        rows = pl.ds((j % per) * rank, rank)
        values.append(pairs[2 * (j // per)][rows, :] + pairs[2 * (j // per) + 1][rows, :])
    for l in reversed(range(local_bits)):
        both = [product(turned(factors[l, j]), split(values[j])) for j in range(nodes)]
        values = [both[j][:rank] + both[j ^ 1 << l][rank:] for j in range(nodes)]
    copies = []
    for j in range(nodes):
        y[j] = product(turned(leaf_in[j]), split(values[j]))
        copies.append(pltpu.make_async_copy(y.at[j], out.at[pl.ds(j * leaf, leaf)], sems.at[j]))
        copies[-1].start()
    for copy in copies:
        copy.wait()


def body(source, leaf_in, factors, leaf_out, weight_table, block_index):
    level_count = factors.shape[0]
    nodes, rank, leaf = leaf_in.shape
    width = source.shape[1]
    f32 = jnp.float32
    local_bits = nodes.bit_length() - 1
    col_size = lax.axis_size("col")
    col_bits = col_size.bit_length() - 1
    where = {}
    for level in range(local_bits, level_count):
        position = level - local_bits
        where[level] = ("col", position) if position < col_bits else ("row", position - col_bits)
    chunks, per = CHUNKS, nodes // CHUNKS
    table_rows = weight_table.shape[0]
    flat = per * rank

    own = lax.axis_index("row") * col_size + lax.axis_index("col")
    place = ((block_index // table_rows) ^ own) * table_rows + block_index % table_rows

    def shape(rows):
        return jax.ShapeDtypeStruct((rows, width), f32)

    unit = 2 * per * rank * 2 * rank * width
    size = 4 * (flat * width * 3 + per * rank * 2 * rank)
    values = list(
        call(
            functools.partial(start_kernel, nodes, rank, leaf, local_bits, chunks),
            [shape(flat + (table_rows if c == 0 else 0)) for c in range(chunks)],
            [HBM, HBM, HBM, VMEM],
            [VMEM] * chunks,
            3 * chunks * unit,
            3 * chunks * size,
            [
                pltpu.VMEM((nodes, leaf, width), f32),
                pltpu.VMEM((nodes, rank, leaf), f32),
                pltpu.VMEM((local_bits, nodes, rank, 2 * rank), f32),
                pltpu.SemaphoreType.DMA((2 * nodes + local_bits,)),
            ],
        )(source, leaf_in, factors, weight_table)
    )
    for level in range(local_bits, level_count - 1):
        got = [exchange(v, *where[level]) for v in values]
        values = [
            call(
                functools.partial(forward_kernel, c * per, per, rank, level),
                shape(2 * values[c].shape[0] - flat),
                [VMEM] * 3,
                VMEM,
                unit,
                size,
            )(values[c], got[c], factors)
            for c in range(chunks)
        ]
    level = level_count - 1
    got = [exchange(v, *where[level]) for v in values]
    pairs = [
        call(
            functools.partial(middle_kernel, c * per, per, rank, level),
            [shape(flat)] * 2,
            [SMEM] + [VMEM] * 6,
            [VMEM] * 2,
            4 * unit,
            2 * size,
        )(place, values[c], got[c], values[0], got[0], factors, leaf_out)
        for c in range(chunks)
    ]
    for level in reversed(range(local_bits, level_count)):
        pairs = [(keep, exchange(send, *where[level])) for keep, send in pairs]
        if level > local_bits:
            pairs = [
                call(
                    functools.partial(backward_kernel, c * per, per, rank, level - 1),
                    [shape(flat)] * 2,
                    [VMEM] * 3,
                    [VMEM] * 2,
                    unit,
                    size,
                )(*pairs[c], factors)
                for c in range(chunks)
            ]
    return call(
        functools.partial(end_kernel, nodes, rank, leaf, local_bits, chunks),
        shape(nodes * leaf),
        [VMEM] * (2 + 2 * chunks),
        HBM,
        3 * chunks * unit,
        3 * chunks * size,
        [pltpu.VMEM((nodes, leaf, width), f32), pltpu.SemaphoreType.DMA((nodes,))],
    )(leaf_in, factors, *[v for pair in pairs for v in pair])


def solution(mesh):
    placed = (
        P(("row", "col"), None),
        P(("row", "col"), None, None),
        P(None, ("row", "col"), None, None),
        P(("row", "col"), None, None),
        P(("row", "col"), None),
        P(("row", "col")),
    )
    return jax.shard_map(
        body, mesh=mesh, in_specs=placed, out_specs=P(("row", "col"), None), check_vma=False
    )
```

```python
import functools

import jax
import jax.numpy as jnp
from jax import lax
from jax.experimental import pallas as pl
from jax.experimental.pallas import tpu as pltpu
from jax.sharding import PartitionSpec as P

MIB = 1 << 20
OFFSET = 1.5
TURN = 1.0
VMEM = pl.BlockSpec(memory_space=pltpu.VMEM)
SMEM = pl.BlockSpec(memory_space=pltpu.SMEM)
HBM = pl.BlockSpec(memory_space=pltpu.HBM)


def exchange(value, axis, bit):
    return lax.ppermute(value, axis, [(i, i ^ 1 << bit) for i in range(lax.axis_size(axis))])


def split(value):
    high = value.astype(jnp.bfloat16)
    return high, (value - high.astype(jnp.float32)).astype(jnp.bfloat16)


def product(a, b):
    one = functools.partial(jnp.dot, preferred_element_type=jnp.float32)
    return one(a[0], b[1]) + one(a[1], b[0]) + one(a[0], b[0])


def turned(value):
    return split(value.T)


def call(kernel, outs, specs, out_specs, flops, traffic, scratch=(), limit=8 * MIB):
    return pl.pallas_call(
        kernel,
        out_shape=outs,
        in_specs=specs,
        out_specs=out_specs,
        scratch_shapes=scratch,
        cost_estimate=pl.CostEstimate(flops=flops, bytes_accessed=traffic, transcendentals=0),
        compiler_params=pltpu.CompilerParams(vmem_limit_bytes=limit),
    )


def lead_kernel(table, out):
    out[...] = table[...]


def start_kernel(nodes, rank, leaf, local_bits, source, leaf_in, factors, table, *rest):
    outs, (x, a, f, sems) = rest[: nodes + 1], rest[nodes + 1 :]
    levels = [pltpu.make_async_copy(factors.at[l], f.at[l], sems.at[2 * nodes + l]) for l in range(local_bits)]
    xs = [pltpu.make_async_copy(source.at[pl.ds(j * leaf, leaf)], x.at[j], sems.at[j]) for j in range(nodes)]
    ins = [pltpu.make_async_copy(leaf_in.at[j], a.at[j], sems.at[nodes + j]) for j in range(nodes)]
    for j in range(nodes):
        ins[j].start()
        xs[j].start()
    for copy in levels:
        copy.start()
    values = []
    for j in range(nodes):
        ins[j].wait()
        xs[j].wait()
        values.append(product(split(a[j]), split(x[j])))
    for l in range(local_bits - 1):
        levels[l].wait()
        halves = [split(v) for v in values]
        values = []
        for j in range(nodes):
            mine, other = halves[j], halves[j ^ 1 << l]
            both = tuple(jnp.concatenate([m, o], axis=0) for m, o in zip(mine, other))
            values.append(product(split(f[l, j]), both))
    levels[-1].wait()
    both = split(jnp.concatenate([values[0], values[nodes // 2]], axis=0))
    outs[0][pl.ds(0, rank), :] = product(split(f[local_bits - 1, 0]), both)
    outs[0][pl.ds(rank, table.shape[0]), :] = table[...]
    for j in range(1, nodes):
        outs[j][...] = values[j]
    outs[nodes][0] = values[0]


def forward_kernel(node, rank, level, own, got, factors, token, out):
    both = split(jnp.concatenate([own[pl.ds(0, rank), :], got[pl.ds(0, rank), :]], axis=0))
    out[pl.ds(0, rank), :] = product(split(factors[level, node]), both)
    extra = out.shape[0] - rank
    if extra:
        half = extra // 2
        out[pl.ds(rank, half), :] = own[pl.ds(rank, half), :]
        out[pl.ds(rank + half, half), :] = got[pl.ds(rank, half), :]


def middle_kernel(node, rank, level, index, own, got, tab_own, tab_got, factors, leaf_out, token, keep, send):
    half = tab_own.shape[0] - rank
    f = factors[level, node]
    both = split(jnp.concatenate([own[pl.ds(0, rank), :], got[pl.ds(0, rank), :]], axis=0))
    value = product(split(f), both)
    l = leaf_out[node]
    image = product(split(l), split(value))
    at = index[node]
    near = rank + jnp.where(at < half, at, at - half)
    weights = jnp.where(at < half, tab_own[pl.ds(near, 1), :], tab_got[pl.ds(near, 1), :])
    value = product(split(l.T * weights), split(image))
    both = product(turned(f), split(value))
    keep[...] = both[:rank]
    send[...] = both[rank:]


def backward_kernel(node, rank, level, own, got, factors, token, keep, send):
    both = product(turned(factors[level, node]), split(own[...] + got[...]))
    keep[...] = both[:rank]
    send[...] = both[rank:]


def end_kernel(nodes, rank, leaf, local_bits, leaf_in, factors, *rest):
    pairs, out, (y, sems) = rest[: 2 * nodes], rest[2 * nodes], rest[2 * nodes + 1 :]
    values = [pairs[2 * j][...] + pairs[2 * j + 1][...] for j in range(nodes)]
    for l in reversed(range(local_bits)):
        both = [product(turned(factors[l, j]), split(values[j])) for j in range(nodes)]
        values = [both[j][:rank] + both[j ^ 1 << l][rank:] for j in range(nodes)]
    copies = []
    for j in range(nodes):
        y[j] = product(turned(leaf_in[j]), split(values[j]))
        copies.append(pltpu.make_async_copy(y.at[j], out.at[pl.ds(j * leaf, leaf)], sems.at[j]))
        copies[-1].start()
    for copy in copies:
        copy.wait()


def task_order(chunks, remote, col_levels):
    times = [2.5 if k == col_levels - 1 else 2.0 if k < col_levels else 0.5 if k == col_levels else 1.5 for k in range(remote)]
    times = times + times[::-1]
    starts = [sum(times[:s]) + (TURN if s >= remote else 0.0) for s in range(2 * remote)]
    tasks = [(c, s) for c in range(chunks) for s in range(2 * remote)]
    return sorted(tasks, key=lambda t: (starts[t[1]] + OFFSET * t[0], -t[1]))


def body(source, leaf_in, factors, leaf_out, weight_table, block_index):
    level_count = factors.shape[0]
    nodes, rank, leaf = leaf_in.shape
    width = source.shape[1]
    f32 = jnp.float32
    local_bits = nodes.bit_length() - 1
    col_size = lax.axis_size("col")
    col_bits = col_size.bit_length() - 1
    remote = level_count - local_bits
    where = {}
    for level in range(local_bits, level_count):
        position = level - local_bits
        where[level] = ("col", position) if position < col_bits else ("row", position - col_bits)
    table_rows = weight_table.shape[0]

    me = lax.axis_index("row") * col_size + lax.axis_index("col")
    place = ((block_index // table_rows) ^ me) * table_rows + block_index % table_rows

    def shape(rows):
        return jax.ShapeDtypeStruct((rows, width), f32)

    unit, size = 1, 1
    rows = call(lead_kernel, shape(table_rows), [VMEM], VMEM, 1 << 33, 1)(weight_table)
    values = list(
        call(
            functools.partial(start_kernel, nodes, rank, leaf, local_bits),
            [shape(rank + (table_rows if c == 0 else 0)) for c in range(nodes)] + [jax.ShapeDtypeStruct((1, rank, width), f32)],
            [HBM, HBM, HBM, VMEM],
            [VMEM] * (nodes + 1),
            2 * nodes * unit,
            2 * nodes * size,
            [
                pltpu.VMEM((nodes, leaf, width), f32),
                pltpu.VMEM((nodes, rank, leaf), f32),
                pltpu.VMEM((local_bits, nodes, rank, 2 * rank), f32),
                pltpu.SemaphoreType.DMA((2 * nodes + local_bits,)),
            ],
        )(source, leaf_in, factors, rows)
    )
    first = values.pop()[0]
    before = [first] + values[1:]
    token = values[0]
    pairs = [None] * nodes
    for c, s in task_order(nodes, remote, col_bits):
        if s == 0:
            level = local_bits
            if c:
                other = c ^ nodes // 2
                values[c] = call(
                    functools.partial(forward_kernel, c, rank, local_bits - 1),
                    shape(rank), [VMEM] * 4, VMEM, unit, size,
                )(before[c], before[other], factors, token)
                token = values[c]
            pairs[c] = (values[c], exchange(values[c], *where[level]))
        elif s < remote:
            level = local_bits + s
            own, got = pairs[c]
            token = call(
                functools.partial(forward_kernel, c, rank, level - 1),
                shape(2 * own.shape[0] - rank), [VMEM] * 4, VMEM, unit, size,
            )(own, got, factors, token)
            pairs[c] = (token, exchange(token, *where[level]))
            if c == 0:
                table = pairs[0]
        else:
            level = level_count - 1 - (s - remote)
            if s == remote:
                keep, send = call(
                    functools.partial(middle_kernel, c, rank, level),
                    [shape(rank)] * 2, [SMEM] + [VMEM] * 7, [VMEM] * 2, 4 * unit, 2 * size,
                )(place, *pairs[c], *table, factors, leaf_out, token)
            else:
                keep, send = call(
                    functools.partial(backward_kernel, c, rank, level),
                    [shape(rank)] * 2, [VMEM] * 4, [VMEM] * 2, unit, size,
                )(*pairs[c], factors, token)
            token = keep
            pairs[c] = (keep, exchange(send, *where[level]))
    return call(
        functools.partial(end_kernel, nodes, rank, leaf, local_bits),
        shape(nodes * leaf),
        [VMEM] * (2 + 2 * nodes),
        HBM,
        3 * nodes * unit,
        3 * nodes * size,
        [pltpu.VMEM((nodes, leaf, width), f32), pltpu.SemaphoreType.DMA((nodes,))],
    )(leaf_in, factors, *[v for pair in pairs for v in pair])


def solution(mesh):
    placed = (
        P(("row", "col"), None),
        P(("row", "col"), None, None),
        P(None, ("row", "col"), None, None),
        P(("row", "col"), None, None),
        P(("row", "col"), None),
        P(("row", "col")),
    )
    return jax.shard_map(
        body, mesh=mesh, in_specs=placed, out_specs=P(("row", "col"), None), check_vma=False
    )
```

```python
import functools

import jax
import jax.numpy as jnp
from jax import lax
from jax.experimental import pallas as pl
from jax.experimental.pallas import tpu as pltpu
from jax.sharding import PartitionSpec as P

MIB = 1 << 20
UNIT = 1 << 26
VMEM = pl.BlockSpec(memory_space=pltpu.VMEM)
SMEM = pl.BlockSpec(memory_space=pltpu.SMEM)
HBM = pl.BlockSpec(memory_space=pltpu.HBM)


def exchange(value, axis, bit):
    return lax.ppermute(value, axis, [(i, i ^ 1 << bit) for i in range(lax.axis_size(axis))])


def split(value):
    high = value.astype(jnp.bfloat16)
    return high, (value - high.astype(jnp.float32)).astype(jnp.bfloat16)


def product(a, b):
    one = functools.partial(jnp.dot, preferred_element_type=jnp.float32)
    return one(a[0], b[1]) + one(a[1], b[0]) + one(a[0], b[0])


def turned(value):
    return split(value.T)


def call(kernel, outs, specs, out_specs, flops, traffic, scratch=(), limit=8 * MIB):
    return pl.pallas_call(
        kernel,
        out_shape=outs,
        in_specs=specs,
        out_specs=out_specs,
        scratch_shapes=scratch,
        cost_estimate=pl.CostEstimate(flops=flops, bytes_accessed=traffic, transcendentals=0),
        compiler_params=pltpu.CompilerParams(vmem_limit_bytes=limit),
    )


def lead_kernel(out):
    out[...] = jnp.zeros_like(out)


def start_kernel(nodes, rank, leaf, local_bits, source, leaf_in, factors, table, lead, *rest):
    outs, (x, a, f, sems) = rest[: nodes + 1], rest[nodes + 1 :]
    levels = [pltpu.make_async_copy(factors.at[l], f.at[l], sems.at[2 * nodes + l]) for l in range(local_bits)]
    xs = [pltpu.make_async_copy(source.at[pl.ds(j * leaf, leaf)], x.at[j], sems.at[j]) for j in range(nodes)]
    ins = [pltpu.make_async_copy(leaf_in.at[j], a.at[j], sems.at[nodes + j]) for j in range(nodes)]
    for j in range(nodes):
        ins[j].start()
        xs[j].start()
    for copy in levels:
        copy.start()
    values = []
    for j in range(nodes):
        ins[j].wait()
        xs[j].wait()
        values.append(product(split(a[j]), split(x[j])))
    for l in range(local_bits - 1):
        levels[l].wait()
        halves = [split(v) for v in values]
        values = []
        for j in range(nodes):
            mine, other = halves[j], halves[j ^ 1 << l]
            both = tuple(jnp.concatenate([m, o], axis=0) for m, o in zip(mine, other))
            values.append(product(split(f[l, j]), both))
    levels[-1].wait()
    both = split(jnp.concatenate([values[0], values[nodes // 2]], axis=0))
    outs[0][pl.ds(0, rank), :] = product(split(f[local_bits - 1, 0]), both)
    outs[0][pl.ds(rank, table.shape[0]), :] = table[...]
    for j in range(1, nodes):
        outs[j][...] = values[j]
    outs[nodes][0] = values[0]


def forward_kernel(node, rank, level, own, got, factors, token, out):
    both = split(jnp.concatenate([own[pl.ds(0, rank), :], got[pl.ds(0, rank), :]], axis=0))
    out[pl.ds(0, rank), :] = product(split(factors[level, node]), both)
    extra = out.shape[0] - rank
    if extra:
        half = extra // 2
        out[pl.ds(rank, half), :] = own[pl.ds(rank, half), :]
        out[pl.ds(rank + half, half), :] = got[pl.ds(rank, half), :]


def middle_kernel(node, rank, level, index, own, got, tab_own, tab_got, factors, leaf_out, token, keep, send):
    half = tab_own.shape[0] - rank
    f = factors[level, node]
    both = split(jnp.concatenate([own[pl.ds(0, rank), :], got[pl.ds(0, rank), :]], axis=0))
    value = product(split(f), both)
    l = leaf_out[node]
    image = product(split(l), split(value))
    at = index[node]
    near = rank + jnp.where(at < half, at, at - half)
    weights = jnp.where(at < half, tab_own[pl.ds(near, 1), :], tab_got[pl.ds(near, 1), :])
    value = product(split(l.T * weights), split(image))
    both = product(turned(f), split(value))
    keep[...] = both[:rank]
    send[...] = both[rank:]


def backward_kernel(node, rank, level, own, got, factors, token, keep, send):
    both = product(turned(factors[level, node]), split(own[...] + got[...]))
    keep[...] = both[:rank]
    send[...] = both[rank:]


def end_kernel(nodes, rank, leaf, local_bits, leaf_in, factors, *rest):
    pairs, out, (y, sems) = rest[: 2 * nodes], rest[2 * nodes], rest[2 * nodes + 1 :]
    values = [pairs[2 * j][...] + pairs[2 * (j ^ nodes // 2) + 1][...] for j in range(nodes)]
    for l in reversed(range(local_bits - 1)):
        both = [product(turned(factors[l, j]), split(values[j])) for j in range(nodes)]
        values = [both[j][:rank] + both[j ^ 1 << l][rank:] for j in range(nodes)]
    copies = []
    for j in range(nodes):
        y[j] = product(turned(leaf_in[j]), split(values[j]))
        copies.append(pltpu.make_async_copy(y.at[j], out.at[pl.ds(j * leaf, leaf)], sems.at[j]))
        copies[-1].start()
    for copy in copies:
        copy.wait()


def task_order(chunks, stages):
    order, queue, waits, entered = [], [], 0, 0
    while len(order) < chunks * stages:
        while entered < chunks and entered <= waits:
            order.append((entered, 0))
            queue.append((entered, 0))
            entered += 1
        c, s = queue.pop(0)
        waits += 1
        if s + 1 < stages:
            order.append((c, s + 1))
            queue.append((c, s + 1))
    return order


def body(source, leaf_in, factors, leaf_out, weight_table, block_index):
    level_count = factors.shape[0]
    nodes, rank, leaf = leaf_in.shape
    width = source.shape[1]
    f32 = jnp.float32
    local_bits = nodes.bit_length() - 1
    col_size = lax.axis_size("col")
    col_bits = col_size.bit_length() - 1
    remote = level_count - local_bits
    where = {}
    for level in range(local_bits, level_count):
        position = level - local_bits
        where[level] = ("col", position) if position < col_bits else ("row", position - col_bits)
    table_rows = weight_table.shape[0]

    me = lax.axis_index("row") * col_size + lax.axis_index("col")
    place = ((block_index // table_rows) ^ me) * table_rows + block_index % table_rows

    def shape(rows):
        return jax.ShapeDtypeStruct((rows, width), f32)

    unit, size = UNIT, 1
    lead = call(lead_kernel, shape(8), [], VMEM, 1 << 33, 1)()
    values = list(
        call(
            functools.partial(start_kernel, nodes, rank, leaf, local_bits),
            [shape(rank + (table_rows if c == 0 else 0)) for c in range(nodes)] + [jax.ShapeDtypeStruct((1, rank, width), f32)],
            [HBM, HBM, HBM, VMEM, VMEM],
            [VMEM] * (nodes + 1),
            2 * nodes * unit,
            2 * nodes * size,
            [
                pltpu.VMEM((nodes, leaf, width), f32),
                pltpu.VMEM((nodes, rank, leaf), f32),
                pltpu.VMEM((local_bits, nodes, rank, 2 * rank), f32),
                pltpu.SemaphoreType.DMA((2 * nodes + local_bits,)),
            ],
        )(source, leaf_in, factors, weight_table, lead)
    )
    first = values.pop()[0]
    before = [first] + values[1:]
    token = values[0]
    pairs = [None] * nodes
    for c, s in task_order(nodes, 2 * remote + 1):
        if s == 0:
            level = local_bits
            if c:
                other = c ^ nodes // 2
                values[c] = call(
                    functools.partial(forward_kernel, c, rank, local_bits - 1),
                    shape(rank), [VMEM] * 4, VMEM, unit, size,
                )(before[c], before[other], factors, token)
                token = values[c]
            pairs[c] = (values[c], exchange(values[c], *where[level]))
        elif s < remote:
            level = local_bits + s
            own, got = pairs[c]
            token = call(
                functools.partial(forward_kernel, c, rank, level - 1),
                shape(2 * own.shape[0] - rank), [VMEM] * 4, VMEM, unit, size,
            )(own, got, factors, token)
            pairs[c] = (token, exchange(token, *where[level]))
            if c == 0:
                table = pairs[0]
        else:
            level = level_count - 1 - (s - remote)
            if s == remote:
                keep, send = call(
                    functools.partial(middle_kernel, c, rank, level),
                    [shape(rank)] * 2, [SMEM] + [VMEM] * 7, [VMEM] * 2, 4 * unit, 2 * size,
                )(place, *pairs[c], *table, factors, leaf_out, token)
            else:
                keep, send = call(
                    functools.partial(backward_kernel, c, rank, level),
                    [shape(rank)] * 2, [VMEM] * 4, [VMEM] * 2, unit, size,
                )(*pairs[c], factors, token)
            token = keep
            pairs[c] = (keep, exchange(send, *where[level]) if level in where else send)
    return call(
        functools.partial(end_kernel, nodes, rank, leaf, local_bits),
        shape(nodes * leaf),
        [VMEM] * (2 + 2 * nodes),
        HBM,
        3 * nodes * unit,
        3 * nodes * size,
        [pltpu.VMEM((nodes, leaf, width), f32), pltpu.SemaphoreType.DMA((nodes,))],
    )(leaf_in, factors, *[v for pair in pairs for v in pair])


def solution(mesh):
    placed = (
        P(("row", "col"), None),
        P(("row", "col"), None, None),
        P(None, ("row", "col"), None, None),
        P(("row", "col"), None, None),
        P(("row", "col"), None),
        P(("row", "col")),
    )
    return jax.shard_map(
        body, mesh=mesh, in_specs=placed, out_specs=P(("row", "col"), None), check_vma=False
    )
```

```python
import functools

import jax
import jax.numpy as jnp
from jax import lax
from jax.experimental import pallas as pl
from jax.experimental.pallas import tpu as pltpu
from jax.sharding import PartitionSpec as P

MIB = 1 << 20
UNIT = 1 << 26
VMEM = pl.BlockSpec(memory_space=pltpu.VMEM)
SMEM = pl.BlockSpec(memory_space=pltpu.SMEM)
HBM = pl.BlockSpec(memory_space=pltpu.HBM)


def exchange(value, axis, bit):
    return lax.ppermute(value, axis, [(i, i ^ 1 << bit) for i in range(lax.axis_size(axis))])


def split(value):
    high = value.astype(jnp.bfloat16)
    return high, (value - high.astype(jnp.float32)).astype(jnp.bfloat16)


def product(a, b):
    one = functools.partial(jnp.dot, preferred_element_type=jnp.float32)
    return one(a[0], b[1]) + one(a[1], b[0]) + one(a[0], b[0])


def turned(value):
    return split(value.T)


def call(kernel, outs, specs, out_specs, flops, traffic, scratch=(), limit=8 * MIB):
    return pl.pallas_call(
        kernel,
        out_shape=outs,
        in_specs=specs,
        out_specs=out_specs,
        scratch_shapes=scratch,
        cost_estimate=pl.CostEstimate(flops=flops, bytes_accessed=traffic, transcendentals=0),
        compiler_params=pltpu.CompilerParams(vmem_limit_bytes=limit),
    )


def lead_kernel(out):
    out[...] = jnp.zeros_like(out)


def start_kernel(nodes, rank, leaf, local_bits, source, leaf_in, factors, table, lead, *rest):
    outs, (x, a, f, sems) = rest[: nodes + 1], rest[nodes + 1 :]
    levels = [pltpu.make_async_copy(factors.at[l], f.at[l], sems.at[2 * nodes + l]) for l in range(local_bits)]
    xs = [pltpu.make_async_copy(source.at[pl.ds(j * leaf, leaf)], x.at[j], sems.at[j]) for j in range(nodes)]
    ins = [pltpu.make_async_copy(leaf_in.at[j], a.at[j], sems.at[nodes + j]) for j in range(nodes)]
    for j in range(nodes):
        ins[j].start()
        xs[j].start()
    for copy in levels:
        copy.start()
    values = []
    for j in range(nodes):
        ins[j].wait()
        xs[j].wait()
        values.append(product(split(a[j]), split(x[j])))
    for l in range(local_bits - 1):
        levels[l].wait()
        halves = [split(v) for v in values]
        values = []
        for j in range(nodes):
            mine, other = halves[j], halves[j ^ 1 << l]
            both = tuple(jnp.concatenate([m, o], axis=0) for m, o in zip(mine, other))
            values.append(product(split(f[l, j]), both))
    levels[-1].wait()
    both = split(jnp.concatenate([values[0], values[nodes // 2]], axis=0))
    outs[0][pl.ds(0, rank), :] = product(split(f[local_bits - 1, 0]), both)
    outs[0][pl.ds(rank, table.shape[0]), :] = table[...]
    for j in range(1, nodes):
        outs[j][...] = values[j]
    outs[nodes][0] = values[0]


def forward_kernel(node, rank, level, own, got, factors, token, out):
    both = split(jnp.concatenate([own[pl.ds(0, rank), :], got[pl.ds(0, rank), :]], axis=0))
    out[pl.ds(0, rank), :] = product(split(factors[level, node]), both)
    extra = out.shape[0] - rank
    if extra:
        half = extra // 2
        out[pl.ds(rank, half), :] = own[pl.ds(rank, half), :]
        out[pl.ds(rank + half, half), :] = got[pl.ds(rank, half), :]


def middle_kernel(node, rank, level, index, own, got, tab_own, tab_got, factors, leaf_out, token, keep, send):
    half = tab_own.shape[0] - rank
    f = factors[level, node]
    both = split(jnp.concatenate([own[pl.ds(0, rank), :], got[pl.ds(0, rank), :]], axis=0))
    value = product(split(f), both)
    l = leaf_out[node]
    image = product(split(l), split(value))
    at = index[node]
    near = rank + jnp.where(at < half, at, at - half)
    weights = jnp.where(at < half, tab_own[pl.ds(near, 1), :], tab_got[pl.ds(near, 1), :])
    value = product(split(l.T * weights), split(image))
    both = product(turned(f), split(value))
    keep[...] = both[:rank]
    send[...] = both[rank:]


def backward_kernel(node, rank, level, own, got, factors, token, keep, send):
    both = product(turned(factors[level, node]), split(own[...] + got[...]))
    keep[...] = both[:rank]
    send[...] = both[rank:]


def end_kernel(nodes, rank, leaf, local_bits, leaf_in, factors, *rest):
    pairs, out, (y, sems) = rest[: 2 * nodes], rest[2 * nodes], rest[2 * nodes + 1 :]
    values = [pairs[2 * j][...] + pairs[2 * (j ^ nodes // 2) + 1][...] for j in range(nodes)]
    for l in reversed(range(local_bits - 1)):
        both = [product(turned(factors[l, j]), split(values[j])) for j in range(nodes)]
        values = [both[j][:rank] + both[j ^ 1 << l][rank:] for j in range(nodes)]
    copies = []
    for j in range(nodes):
        y[j] = product(turned(leaf_in[j]), split(values[j]))
        copies.append(pltpu.make_async_copy(y.at[j], out.at[pl.ds(j * leaf, leaf)], sems.at[j]))
        copies[-1].start()
    for copy in copies:
        copy.wait()


def task_order(chunks, stages):
    order, queue, waits, entered = [], [], 0, 0
    while len(order) < chunks * stages:
        while entered < chunks and entered * (entered + 1) // 4 <= waits:
            order.append((entered, 0))
            queue.append((entered, 0))
            entered += 1
        c, s = queue.pop(0)
        waits += 1
        if s + 1 < stages:
            order.append((c, s + 1))
            queue.append((c, s + 1))
    return order


def body(source, leaf_in, factors, leaf_out, weight_table, block_index):
    level_count = factors.shape[0]
    nodes, rank, leaf = leaf_in.shape
    width = source.shape[1]
    f32 = jnp.float32
    local_bits = nodes.bit_length() - 1
    col_size = lax.axis_size("col")
    col_bits = col_size.bit_length() - 1
    remote = level_count - local_bits
    where = {}
    for level in range(local_bits, level_count):
        position = level - local_bits
        where[level] = ("col", position) if position < col_bits else ("row", position - col_bits)
    table_rows = weight_table.shape[0]

    me = lax.axis_index("row") * col_size + lax.axis_index("col")
    place = ((block_index // table_rows) ^ me) * table_rows + block_index % table_rows

    def shape(rows):
        return jax.ShapeDtypeStruct((rows, width), f32)

    unit, size = UNIT, 1
    lead = call(lead_kernel, shape(8), [], VMEM, 1 << 33, 1)()
    values = list(
        call(
            functools.partial(start_kernel, nodes, rank, leaf, local_bits),
            [shape(rank + (table_rows if c == 0 else 0)) for c in range(nodes)] + [jax.ShapeDtypeStruct((1, rank, width), f32)],
            [HBM, HBM, HBM, VMEM, VMEM],
            [VMEM] * (nodes + 1),
            2 * nodes * unit,
            2 * nodes * size,
            [
                pltpu.VMEM((nodes, leaf, width), f32),
                pltpu.VMEM((nodes, rank, leaf), f32),
                pltpu.VMEM((local_bits, nodes, rank, 2 * rank), f32),
                pltpu.SemaphoreType.DMA((2 * nodes + local_bits,)),
            ],
        )(source, leaf_in, factors, weight_table, lead)
    )
    first = values.pop()[0]
    before = [first] + values[1:]
    token = values[0]
    pairs = [None] * nodes
    for c, s in task_order(nodes, 2 * remote + 1):
        if s == 0:
            level = local_bits
            if c:
                other = c ^ nodes // 2
                values[c] = call(
                    functools.partial(forward_kernel, c, rank, local_bits - 1),
                    shape(rank), [VMEM] * 4, VMEM, unit, size,
                )(before[c], before[other], factors, token)
                token = values[c]
            pairs[c] = (values[c], exchange(values[c], *where[level]))
        elif s < remote:
            level = local_bits + s
            own, got = pairs[c]
            token = call(
                functools.partial(forward_kernel, c, rank, level - 1),
                shape(2 * own.shape[0] - rank), [VMEM] * 4, VMEM, unit, size,
            )(own, got, factors, token)
            pairs[c] = (token, exchange(token, *where[level]))
            if c == 0:
                table = pairs[0]
        else:
            level = level_count - 1 - (s - remote)
            if s == remote:
                keep, send = call(
                    functools.partial(middle_kernel, c, rank, level),
                    [shape(rank)] * 2, [SMEM] + [VMEM] * 7, [VMEM] * 2, 4 * unit, 2 * size,
                )(place, *pairs[c], *table, factors, leaf_out, token)
            else:
                keep, send = call(
                    functools.partial(backward_kernel, c, rank, level),
                    [shape(rank)] * 2, [VMEM] * 4, [VMEM] * 2, unit, size,
                )(*pairs[c], factors, token)
            token = keep
            pairs[c] = (keep, exchange(send, *where[level]) if level in where else send)
    return call(
        functools.partial(end_kernel, nodes, rank, leaf, local_bits),
        shape(nodes * leaf),
        [VMEM] * (2 + 2 * nodes),
        HBM,
        3 * nodes * unit,
        3 * nodes * size,
        [pltpu.VMEM((nodes, leaf, width), f32), pltpu.SemaphoreType.DMA((nodes,))],
    )(leaf_in, factors, *[v for pair in pairs for v in pair])


def solution(mesh):
    placed = (
        P(("row", "col"), None),
        P(("row", "col"), None, None),
        P(None, ("row", "col"), None, None),
        P(("row", "col"), None, None),
        P(("row", "col"), None),
        P(("row", "col")),
    )
    return jax.shard_map(
        body, mesh=mesh, in_specs=placed, out_specs=P(("row", "col"), None), check_vma=False
    )
```

```python
import functools

import jax
import jax.numpy as jnp
from jax import lax
from jax.experimental import pallas as pl
from jax.experimental.pallas import tpu as pltpu
from jax.sharding import PartitionSpec as P

MIB = 1 << 20
UNIT = 1 << 26
GAIN = 1 << 25
VMEM = pl.BlockSpec(memory_space=pltpu.VMEM)
SMEM = pl.BlockSpec(memory_space=pltpu.SMEM)
HBM = pl.BlockSpec(memory_space=pltpu.HBM)


def exchange(value, axis, bit):
    return lax.ppermute(value, axis, [(i, i ^ 1 << bit) for i in range(lax.axis_size(axis))])


def split(value):
    high = value.astype(jnp.bfloat16)
    return high, (value - high.astype(jnp.float32)).astype(jnp.bfloat16)


def product(a, b):
    one = functools.partial(jnp.dot, preferred_element_type=jnp.float32)
    return one(a[0], b[1]) + one(a[1], b[0]) + one(a[0], b[0])


def product_turned(a, b):
    one = functools.partial(
        lax.dot_general, dimension_numbers=(((0,), (0,)), ((), ())), preferred_element_type=jnp.float32
    )
    return one(a[0], b[1]) + one(a[1], b[0]) + one(a[0], b[0])


def picked(hot, table):
    total, rest = 0.0, table
    for _ in range(3):
        part = rest.astype(jnp.bfloat16)
        rest = rest - part.astype(jnp.float32)
        total = total + jnp.dot(hot.astype(jnp.bfloat16), part, preferred_element_type=jnp.float32)
    return total


def call(kernel, outs, specs, out_specs, flops, traffic, scratch=(), limit=8 * MIB):
    return pl.pallas_call(
        kernel,
        out_shape=outs,
        in_specs=specs,
        out_specs=out_specs,
        scratch_shapes=scratch,
        cost_estimate=pl.CostEstimate(flops=flops, bytes_accessed=traffic, transcendentals=0),
        compiler_params=pltpu.CompilerParams(vmem_limit_bytes=limit),
    )


def lead_kernel(out):
    out[...] = jnp.zeros_like(out)


def halves(mine, value):
    width = value.shape[1] // 2
    left, right = value[:, :width], value[:, width:]
    return jnp.where(mine, left, right), jnp.where(mine, right, left)


def leading():
    return lax.rem(lax.axis_index("row"), 2) == 0


def stacked(a, b):
    return split(jnp.concatenate([a, b], axis=0))


def start_kernel(nodes, rank, leaf, local_bits, source, leaf_in, factors, table, lead, mid, keep, send, x, a, f, sems):
    levels = [pltpu.make_async_copy(factors.at[l], f.at[l], sems.at[2 * nodes + l]) for l in range(local_bits)]
    xs = [pltpu.make_async_copy(source.at[pl.ds(j * leaf, leaf)], x.at[j], sems.at[j]) for j in range(nodes)]
    ins = [pltpu.make_async_copy(leaf_in.at[j], a.at[j], sems.at[nodes + j]) for j in range(nodes)]
    for j in range(nodes):
        ins[j].start()
        xs[j].start()
    for copy in levels:
        copy.start()
    values = []
    for j in range(nodes):
        ins[j].wait()
        xs[j].wait()
        values.append(product(split(a[j]), split(x[j])))
    for l in range(local_bits - 1):
        levels[l].wait()
        parts = [split(v) for v in values]
        values = []
        for j in range(nodes):
            mine, other = parts[j], parts[j ^ 1 << l]
            both = tuple(jnp.concatenate([m, o], axis=0) for m, o in zip(mine, other))
            values.append(product(split(f[l, j]), both))
    for j in range(nodes):
        mid[j] = values[j]
    levels[-1].wait()
    mine = leading()
    for j in range(nodes // 2):
        value = product(split(f[local_bits - 1, j]), stacked(values[j], values[j ^ nodes // 2]))
        rows = pl.ds(j * rank, rank)
        keep[rows, :], send[rows, :] = halves(mine, value)
    rows, half = table.shape[0], keep.shape[1]
    for k in range(table.shape[1] // half):
        tail = pl.ds(nodes // 2 * rank + k * rows, rows)
        keep[tail, :] = table[:, k * half : (k + 1) * half]
        send[tail, :] = table[:, k * half : (k + 1) * half]


def second_kernel(nodes, rank, level, mid, factors, token, keep, send):
    mine = leading()
    for j in range(nodes // 2):
        node = nodes // 2 + j
        value = product(split(factors[level, node]), stacked(mid[node], mid[j]))
        rows = pl.ds(j * rank, rank)
        keep[rows, :], send[rows, :] = halves(mine, value)


def index_kernel(rows_each, ways, col_size, bits, index, other_index, token, hot):
    me = lax.axis_index("row") * col_size + lax.axis_index("col")
    lane = lax.broadcasted_iota(jnp.int32, (1, hot.shape[1]), 1)
    nodes = index.shape[0]
    for j in range(2 * nodes):
        at = index[j] if j < nodes else other_index[j - nodes]
        differs = lax.div(at, rows_each) ^ me
        place = jnp.int32(0)
        for count, bit in enumerate(bits):
            place = place | (((differs >> bit) & 1) << count)
        place = place * (rows_each * ways) + lax.rem(at, rows_each)
        for k in range(ways):
            hot[pl.ds(k * 2 * nodes + j, 1), :] = (lane == place + k * rows_each).astype(jnp.float32)


def enter_kernel(at, rank, extra, from_row, keep, got, token, out):
    out[pl.ds(0, rank), :] = keep[pl.ds(at * rank, rank), :]
    out[pl.ds(rank, rank), :] = got[pl.ds(at * rank, rank), :]
    if extra:
        out[pl.ds(2 * rank, extra), :] = keep[pl.ds(from_row, extra), :]
        out[pl.ds(2 * rank + extra, extra), :] = got[pl.ds(from_row, extra), :]


def forward_kernel(node, rank, level, core, own, got, factors, others, token, out):
    top, low = pl.ds(0, rank), pl.ds(rank, rank)
    first = product(split(factors[level, node]), stacked(own[top, :], got[top, :]))
    second = product(split(others[level, node]), stacked(own[low, :], got[low, :]))
    if core:
        first, second = (
            product(split(factors[level + 1, node]), stacked(first, second)),
            product(split(others[level + 1, node]), stacked(second, first)),
        )
    out[top, :] = first
    out[low, :] = second
    extra = own.shape[0] - 2 * rank
    if extra:
        out[pl.ds(2 * rank, extra), :] = own[pl.ds(2 * rank, extra), :]
        out[pl.ds(2 * rank + extra, extra), :] = got[pl.ds(2 * rank, extra), :]


def middle_kernel(node, nodes, rank, level, hot, own, got, tab_own, tab_got, factors, others, leaf_out, other_out, token, keep, send):
    extra = tab_own.shape[0] - 2 * rank
    tail = pl.ds(2 * rank, extra)
    table = jnp.concatenate([tab_own[tail, :], tab_got[tail, :]], axis=0)
    rows = picked(hot[...], table)
    for k, (fs, ls) in enumerate(((factors, leaf_out), (others, other_out))):
        here = pl.ds(k * rank, rank)
        f, l = split(fs[level, node]), ls[node]
        value = product(f, stacked(own[here, :], got[here, :]))
        at = k * nodes + node
        weights = jnp.concatenate([rows[at : at + 1], rows[2 * nodes + at : 2 * nodes + at + 1]], axis=1)
        value = product(split(product(split(l.T * weights), split(l))), split(value))
        both = product_turned(f, split(value))
        keep[here, :] = both[:rank]
        send[here, :] = both[rank:]


def backward_kernel(node, rank, level, core, own, got, factors, others, token, keep, send):
    top, low = pl.ds(0, rank), pl.ds(rank, rank)
    first, second = own[top, :] + got[top, :], own[low, :] + got[low, :]
    if core:
        one = product_turned(split(factors[level + 1, node]), split(first))
        two = product_turned(split(others[level + 1, node]), split(second))
        first, second = one[:rank] + two[rank:], two[:rank] + one[rank:]
    one = product_turned(split(factors[level, node]), split(first))
    two = product_turned(split(others[level, node]), split(second))
    keep[top, :], send[top, :] = one[:rank], one[rank:]
    keep[low, :], send[low, :] = two[:rank], two[rank:]


def leave_kernel(rank, own, got, token, keep, send):
    keep[...] = own[pl.ds(0, rank), :] + got[pl.ds(0, rank), :]
    send[...] = own[pl.ds(rank, rank), :] + got[pl.ds(rank, rank), :]


def home_kernel(node, rank, level, own, got, factors, token, keep, send):
    mine = leading()
    a, b = own[...], got[...]
    value = jnp.concatenate([jnp.where(mine, a, b), jnp.where(mine, b, a)], axis=1)
    both = product_turned(split(factors[level, node]), split(value))
    keep[...] = both[:rank]
    send[...] = both[rank:]


def end_kernel(nodes, rank, leaf, local_bits, leaf_in, factors, *rest):
    pairs, out, (y, sems) = rest[: 2 * nodes], rest[2 * nodes], rest[2 * nodes + 1 :]
    values = [pairs[2 * j][...] + pairs[2 * (j ^ nodes // 2) + 1][...] for j in range(nodes)]
    for l in reversed(range(local_bits - 1)):
        both = [product_turned(split(factors[l, j]), split(values[j])) for j in range(nodes)]
        values = [both[j][:rank] + both[j ^ 1 << l][rank:] for j in range(nodes)]
    copies = []
    for j in range(nodes):
        y[j] = product_turned(split(leaf_in[j]), split(values[j]))
        copies.append(pltpu.make_async_copy(y.at[j], out.at[pl.ds(j * leaf, leaf)], sems.at[j]))
        copies[-1].start()
    for copy in copies:
        copy.wait()


def task_order(chunks, stages):
    order, queue, waits, entered = [], [], 0, 0
    while len(order) < chunks * stages:
        while entered < chunks and entered * (entered + 1) // 4 <= waits:
            order.append((entered, 0))
            queue.append((entered, 0))
            entered += 1
        c, s = queue.pop(0)
        waits += 1
        if s + 1 < stages:
            order.append((c, s + 1))
            queue.append((c, s + 1))
    return order


def body(source, leaf_in, factors, leaf_out, weight_table, block_index):
    level_count = factors.shape[0]
    nodes, rank, leaf = leaf_in.shape
    width = source.shape[1]
    f32 = jnp.float32
    local_bits = nodes.bit_length() - 1
    col_size = lax.axis_size("col")
    col_bits = col_size.bit_length() - 1
    core_level = local_bits + col_bits
    chain = [level for level in range(local_bits, level_count) if level != core_level]
    steps = len(chain)
    half = width // 2
    ways = leaf // half
    table_rows = weight_table.shape[0] * ways

    def along(level, value):
        position = level - local_bits
        return exchange(value, "col", position) if position < col_bits else exchange(value, "row", position - col_bits)

    others, other_out, other_index = (along(core_level, v) for v in (factors, leaf_out, block_index))

    def shape(rows, columns=half):
        return jax.ShapeDtypeStruct((rows, columns), f32)

    unit, size = UNIT, 1
    lead = call(lead_kernel, shape(8), [], VMEM, 1 << 33, 1)()
    entry = nodes // 2 * rank
    mid, keep_a, send_a = call(
        functools.partial(start_kernel, nodes, rank, leaf, local_bits),
        [jax.ShapeDtypeStruct((nodes, rank, width), f32)] + [shape(entry + table_rows)] * 2,
        [HBM, HBM, HBM, VMEM, VMEM],
        [VMEM] * 3,
        2 * nodes * unit,
        2 * nodes * size,
        [
            pltpu.VMEM((nodes, leaf, width), f32),
            pltpu.VMEM((nodes, rank, leaf), f32),
            pltpu.VMEM((local_bits, nodes, rank, 2 * rank), f32),
            pltpu.SemaphoreType.DMA((2 * nodes + local_bits,)),
        ],
    )(source, leaf_in, factors, weight_table, lead)
    got_a = along(core_level, send_a)
    keep_b, send_b = call(
        functools.partial(second_kernel, nodes, rank, local_bits - 1),
        [shape(entry)] * 2, [VMEM] * 3, [VMEM] * 2, unit, size,
    )(mid, factors, keep_a)
    got_b = along(core_level, send_b)
    hot = call(
        functools.partial(index_kernel, weight_table.shape[0], ways, col_size, [k - local_bits for k in [core_level] + chain]),
        shape(2 * nodes * ways, table_rows << (steps + 1)), [SMEM, SMEM, VMEM], VMEM, unit, size,
    )(block_index, other_index, keep_b)
    token = hot
    pairs = [None] * nodes
    order = task_order(nodes, 2 * steps + 2)
    for (c, s), after in zip(order, order[1:] + [(1, 0)]):
        unit = UNIT + (GAIN * max(pairs[0][0].shape[0] - 2 * rank, 0) // 2 if after[0] == 0 and after[1] > 0 else 0)
        level = chain[s] if s < steps else chain[2 * steps - 1 - s] if s < 2 * steps else None
        if s == 0:
            extra = table_rows if c == 0 else 0
            keep, got = (keep_a, got_a) if c < nodes // 2 else (keep_b, got_b)
            token = call(
                functools.partial(enter_kernel, c % (nodes // 2), rank, extra, entry),
                shape(2 * rank + 2 * extra), [VMEM] * 3, VMEM, unit, size,
            )(keep, got, token)
            pairs[c] = (token, along(level, token))
        elif s < steps:
            own, got = pairs[c]
            token = call(
                functools.partial(forward_kernel, c, rank, chain[s - 1], chain[s - 1] + 1 == core_level),
                shape(2 * own.shape[0] - 2 * rank), [VMEM] * 5, VMEM, unit, size,
            )(own, got, factors, others, token)
            pairs[c] = (token, along(level, token))
            if c == 0:
                gathered = pairs[0]
        elif s == 2 * steps + 1:
            token, send = call(
                functools.partial(home_kernel, c, rank, local_bits - 1),
                [shape(rank, width)] * 2, [VMEM] * 4, [VMEM] * 2, unit, size,
            )(*pairs[c], factors, token)
            pairs[c] = (token, send)
        else:
            if s == steps:
                token, send = call(
                    functools.partial(middle_kernel, c, nodes, rank, level),
                    [shape(2 * rank)] * 2, [VMEM] * 10, [VMEM] * 2, unit, size,
                )(hot, *pairs[c], *gathered, factors, others, leaf_out, other_out, token)
            elif s < 2 * steps:
                token, send = call(
                    functools.partial(backward_kernel, c, rank, level, level + 1 == core_level),
                    [shape(2 * rank)] * 2, [VMEM] * 5, [VMEM] * 2, unit, size,
                )(*pairs[c], factors, others, token)
            else:
                level = core_level
                token, send = call(
                    functools.partial(leave_kernel, rank), [shape(rank)] * 2, [VMEM] * 3, [VMEM] * 2, unit, size
                )(*pairs[c], token)
            pairs[c] = (token, along(level, send))
    return call(
        functools.partial(end_kernel, nodes, rank, leaf, local_bits),
        shape(nodes * leaf, width),
        [VMEM] * (2 + 2 * nodes),
        HBM,
        3 * nodes * unit,
        3 * nodes * size,
        [pltpu.VMEM((nodes, leaf, width), f32), pltpu.SemaphoreType.DMA((nodes,))],
    )(leaf_in, factors, *[v for pair in pairs for v in pair])


def solution(mesh):
    placed = (
        P(("row", "col"), None),
        P(("row", "col"), None, None),
        P(None, ("row", "col"), None, None),
        P(("row", "col"), None, None),
        P(("row", "col"), None),
        P(("row", "col")),
    )
    return jax.shard_map(
        body, mesh=mesh, in_specs=placed, out_specs=P(("row", "col"), None), check_vma=False
    )
```

```python
import functools

import jax
import jax.numpy as jnp
from jax import lax
from jax.experimental import pallas as pl
from jax.experimental.pallas import tpu as pltpu
from jax.sharding import PartitionSpec as P

MIB = 1 << 20
UNIT = 1 << 26
GAIN = 1 << 25
VMEM = pl.BlockSpec(memory_space=pltpu.VMEM)
SMEM = pl.BlockSpec(memory_space=pltpu.SMEM)
HBM = pl.BlockSpec(memory_space=pltpu.HBM)


def exchange(value, axis, bit):
    return lax.ppermute(value, axis, [(i, i ^ 1 << bit) for i in range(lax.axis_size(axis))])


def split(value):
    high = value.astype(jnp.bfloat16)
    return high, (value - high.astype(jnp.float32)).astype(jnp.bfloat16)


def product(a, b):
    one = functools.partial(jnp.dot, preferred_element_type=jnp.float32)
    return one(a[0], b[1]) + one(a[1], b[0]) + one(a[0], b[0])


def product_turned(a, b):
    one = functools.partial(
        lax.dot_general, dimension_numbers=(((0,), (0,)), ((), ())), preferred_element_type=jnp.float32
    )
    return one(a[0], b[1]) + one(a[1], b[0]) + one(a[0], b[0])


def picked(hot, table):
    total, rest = 0.0, table
    for _ in range(3):
        part = rest.astype(jnp.bfloat16)
        rest = rest - part.astype(jnp.float32)
        total = total + jnp.dot(hot.astype(jnp.bfloat16), part, preferred_element_type=jnp.float32)
    return total


def call(kernel, outs, specs, out_specs, flops, traffic, scratch=(), limit=8 * MIB):
    return pl.pallas_call(
        kernel,
        out_shape=outs,
        in_specs=specs,
        out_specs=out_specs,
        scratch_shapes=scratch,
        cost_estimate=pl.CostEstimate(flops=flops, bytes_accessed=traffic, transcendentals=0),
        compiler_params=pltpu.CompilerParams(vmem_limit_bytes=limit),
    )


def lead_kernel(out):
    out[...] = jnp.zeros_like(out)


def halves(mine, value):
    width = value.shape[1] // 2
    left, right = value[:, :width], value[:, width:]
    return jnp.where(mine, left, right), jnp.where(mine, right, left)


def leading():
    return lax.rem(lax.axis_index("row"), 2) == 0


def stacked(a, b):
    return split(jnp.concatenate([a, b], axis=0))


def start_kernel(nodes, rank, leaf, local_bits, source, leaf_in, factors, table, lead, mid, keep, send, x, a, f, sems):
    levels = [pltpu.make_async_copy(factors.at[l], f.at[l], sems.at[2 * nodes + l]) for l in range(local_bits)]
    xs = [pltpu.make_async_copy(source.at[pl.ds(j * leaf, leaf)], x.at[j], sems.at[j]) for j in range(nodes)]
    ins = [pltpu.make_async_copy(leaf_in.at[j], a.at[j], sems.at[nodes + j]) for j in range(nodes)]
    for j in range(nodes):
        ins[j].start()
        xs[j].start()
    for copy in levels:
        copy.start()
    values = []
    for j in range(nodes):
        ins[j].wait()
        xs[j].wait()
        values.append(product(split(a[j]), split(x[j])))
    for l in range(local_bits - 1):
        levels[l].wait()
        parts = [split(v) for v in values]
        values = []
        for j in range(nodes):
            mine, other = parts[j], parts[j ^ 1 << l]
            both = tuple(jnp.concatenate([m, o], axis=0) for m, o in zip(mine, other))
            values.append(product(split(f[l, j]), both))
    for j in range(nodes):
        mid[j] = values[j]
    levels[-1].wait()
    mine = leading()
    for j in range(nodes // 2):
        value = product(split(f[local_bits - 1, j]), stacked(values[j], values[j ^ nodes // 2]))
        rows = pl.ds(j * rank, rank)
        keep[rows, :], send[rows, :] = halves(mine, value)
    rows, half = table.shape[0], keep.shape[1]
    for k in range(table.shape[1] // half):
        tail = pl.ds(nodes // 2 * rank + k * rows, rows)
        keep[tail, :] = table[:, k * half : (k + 1) * half]
        send[tail, :] = table[:, k * half : (k + 1) * half]


def second_kernel(nodes, rank, level, mid, factors, token, keep, send):
    mine = leading()
    for j in range(nodes // 2):
        node = nodes // 2 + j
        value = product(split(factors[level, node]), stacked(mid[node], mid[j]))
        rows = pl.ds(j * rank, rank)
        keep[rows, :], send[rows, :] = halves(mine, value)


def index_kernel(rows_each, ways, col_size, bits, index, other_index, token, hot):
    me = lax.axis_index("row") * col_size + lax.axis_index("col")
    lane = lax.broadcasted_iota(jnp.int32, (1, hot.shape[1]), 1)
    nodes = index.shape[0]
    for j in range(2 * nodes):
        at = index[j] if j < nodes else other_index[j - nodes]
        differs = lax.div(at, rows_each) ^ me
        place = jnp.int32(0)
        for count, bit in enumerate(bits):
            place = place | (((differs >> bit) & 1) << count)
        place = place * (rows_each * ways) + lax.rem(at, rows_each)
        for k in range(ways):
            hot[pl.ds(k * 2 * nodes + j, 1), :] = (lane == place + k * rows_each).astype(jnp.float32)


def enter_kernel(at, rank, extra, from_row, keep, got, token, out):
    out[pl.ds(0, rank), :] = keep[pl.ds(at * rank, rank), :]
    out[pl.ds(rank, rank), :] = got[pl.ds(at * rank, rank), :]
    if extra:
        out[pl.ds(2 * rank, extra), :] = keep[pl.ds(from_row, extra), :]
        out[pl.ds(2 * rank + extra, extra), :] = got[pl.ds(from_row, extra), :]


def forward_kernel(node, rank, level, core, own, got, factors, others, token, out):
    top, low = pl.ds(0, rank), pl.ds(rank, rank)
    first = product(split(factors[level, node]), stacked(own[top, :], got[top, :]))
    second = product(split(others[level, node]), stacked(own[low, :], got[low, :]))
    if core:
        first, second = (
            product(split(factors[level + 1, node]), stacked(first, second)),
            product(split(others[level + 1, node]), stacked(second, first)),
        )
    out[top, :] = first
    out[low, :] = second
    extra = own.shape[0] - 2 * rank
    if extra:
        out[pl.ds(2 * rank, extra), :] = own[pl.ds(2 * rank, extra), :]
        out[pl.ds(2 * rank + extra, extra), :] = got[pl.ds(2 * rank, extra), :]


def middle_kernel(node, nodes, rank, level, hot, own, got, tab_own, tab_got, factors, others, leaf_out, other_out, token, keep, send):
    extra = tab_own.shape[0] - 2 * rank
    tail = pl.ds(2 * rank, extra)
    table = jnp.concatenate([tab_own[tail, :], tab_got[tail, :]], axis=0)
    rows = picked(hot[...], table)
    for k, (fs, ls) in enumerate(((factors, leaf_out), (others, other_out))):
        here = pl.ds(k * rank, rank)
        f, l = split(fs[level, node]), ls[node]
        value = product(f, stacked(own[here, :], got[here, :]))
        at = k * nodes + node
        weights = jnp.concatenate([rows[at : at + 1], rows[2 * nodes + at : 2 * nodes + at + 1]], axis=1)
        value = product(split(product(split(l.T * weights), split(l))), split(value))
        both = product_turned(f, split(value))
        keep[here, :] = both[:rank]
        send[here, :] = both[rank:]


def backward_kernel(node, rank, level, core, own, got, factors, others, token, keep, send):
    top, low = pl.ds(0, rank), pl.ds(rank, rank)
    first, second = own[top, :] + got[top, :], own[low, :] + got[low, :]
    if core:
        one = product_turned(split(factors[level + 1, node]), split(first))
        two = product_turned(split(others[level + 1, node]), split(second))
        first, second = one[:rank] + two[rank:], two[:rank] + one[rank:]
    one = product_turned(split(factors[level, node]), split(first))
    two = product_turned(split(others[level, node]), split(second))
    keep[top, :], send[top, :] = one[:rank], one[rank:]
    keep[low, :], send[low, :] = two[:rank], two[rank:]


def leave_kernel(rank, own, got, token, keep, send):
    keep[...] = own[pl.ds(0, rank), :] + got[pl.ds(0, rank), :]
    send[pl.ds(0, rank), :] = own[pl.ds(rank, rank), :] + got[pl.ds(rank, rank), :]
    send[pl.ds(rank, rank), :] = jnp.zeros((rank, send.shape[1]), jnp.float32)


def home_kernel(node, rank, level, own, got, factors, token, keep, send):
    mine = leading()
    a, b = own[...], got[pl.ds(0, rank), :]
    value = jnp.concatenate([jnp.where(mine, a, b), jnp.where(mine, b, a)], axis=1)
    both = product_turned(split(factors[level, node]), split(value))
    keep[...] = both[:rank]
    send[...] = both[rank:]


def end_kernel(nodes, rank, leaf, local_bits, leaf_in, factors, *rest):
    pairs, out, (y, sems) = rest[: 2 * nodes], rest[2 * nodes], rest[2 * nodes + 1 :]
    values = [pairs[2 * j][...] + pairs[2 * (j ^ nodes // 2) + 1][...] for j in range(nodes)]
    for l in reversed(range(local_bits - 1)):
        both = [product_turned(split(factors[l, j]), split(values[j])) for j in range(nodes)]
        values = [both[j][:rank] + both[j ^ 1 << l][rank:] for j in range(nodes)]
    copies = []
    for j in range(nodes):
        y[j] = product_turned(split(leaf_in[j]), split(values[j]))
        copies.append(pltpu.make_async_copy(y.at[j], out.at[pl.ds(j * leaf, leaf)], sems.at[j]))
        copies[-1].start()
    for copy in copies:
        copy.wait()


def task_order(chunks, stages):
    order, queue, waits, entered = [], [], 0, 0
    while len(order) < chunks * stages:
        while entered < chunks and entered <= waits + 1:
            order.append((entered, 0))
            queue.append((entered, 0))
            entered += 1
        c, s = queue.pop(0)
        waits += 1
        if s + 1 < stages:
            order.append((c, s + 1))
            queue.append((c, s + 1))
    return order


def body(source, leaf_in, factors, leaf_out, weight_table, block_index):
    level_count = factors.shape[0]
    nodes, rank, leaf = leaf_in.shape
    width = source.shape[1]
    f32 = jnp.float32
    local_bits = nodes.bit_length() - 1
    col_size = lax.axis_size("col")
    col_bits = col_size.bit_length() - 1
    core_level = local_bits + col_bits
    chain = [level for level in range(local_bits, level_count) if level != core_level]
    steps = len(chain)
    half = width // 2
    ways = leaf // half
    table_rows = weight_table.shape[0] * ways

    def along(level, value):
        position = level - local_bits
        return exchange(value, "col", position) if position < col_bits else exchange(value, "row", position - col_bits)

    others, other_out, other_index = (along(core_level, v) for v in (factors, leaf_out, block_index))

    def shape(rows, columns=half):
        return jax.ShapeDtypeStruct((rows, columns), f32)

    unit, size = UNIT, 1
    lead = call(lead_kernel, shape(8), [], VMEM, 1 << 33, 1)()
    entry = nodes // 2 * rank
    mid, keep_a, send_a = call(
        functools.partial(start_kernel, nodes, rank, leaf, local_bits),
        [jax.ShapeDtypeStruct((nodes, rank, width), f32)] + [shape(entry + table_rows)] * 2,
        [HBM, HBM, HBM, VMEM, VMEM],
        [VMEM] * 3,
        2 * nodes * unit,
        2 * nodes * size,
        [
            pltpu.VMEM((nodes, leaf, width), f32),
            pltpu.VMEM((nodes, rank, leaf), f32),
            pltpu.VMEM((local_bits, nodes, rank, 2 * rank), f32),
            pltpu.SemaphoreType.DMA((2 * nodes + local_bits,)),
        ],
    )(source, leaf_in, factors, weight_table, lead)
    got_a = along(core_level, send_a)
    keep_b, send_b = call(
        functools.partial(second_kernel, nodes, rank, local_bits - 1),
        [shape(entry)] * 2, [VMEM] * 3, [VMEM] * 2, unit, size,
    )(mid, factors, keep_a)
    got_b = along(core_level, send_b)
    token = keep_b
    pairs = [None] * nodes
    order = task_order(nodes, 2 * steps + 2)
    for (c, s), after in zip(order, order[1:] + [(1, 0)]):
        unit = UNIT + (GAIN * max(pairs[0][0].shape[0] - 2 * rank, 0) // 2 if after[0] == 0 and after[1] > 0 and s + c > 0 else 0)
        level = chain[s] if s < steps else chain[2 * steps - 1 - s] if s < 2 * steps else None
        if s == 0:
            extra = table_rows if c == 0 else 0
            keep, got = (keep_a, got_a) if c < nodes // 2 else (keep_b, got_b)
            token = call(
                functools.partial(enter_kernel, c % (nodes // 2), rank, extra, entry),
                shape(2 * rank + 2 * extra), [VMEM] * 3, VMEM, unit, size,
            )(keep, got, token)
            pairs[c] = (token, along(level, token))
            if c == 1:
                hot = call(
                    functools.partial(
                        index_kernel, weight_table.shape[0], ways, col_size, [k - local_bits for k in [core_level] + chain]
                    ),
                    shape(2 * nodes * ways, table_rows << (steps + 1)), [SMEM, SMEM, VMEM], VMEM, unit, size,
                )(block_index, other_index, token)
                token = hot
        elif s < steps:
            own, got = pairs[c]
            token = call(
                functools.partial(forward_kernel, c, rank, chain[s - 1], chain[s - 1] + 1 == core_level),
                shape(2 * own.shape[0] - 2 * rank), [VMEM] * 5, VMEM, unit, size,
            )(own, got, factors, others, token)
            pairs[c] = (token, along(level, token))
            if c == 0:
                gathered = pairs[0]
        elif s == 2 * steps + 1:
            token, send = call(
                functools.partial(home_kernel, c, rank, local_bits - 1),
                [shape(rank, width)] * 2, [VMEM] * 4, [VMEM] * 2, unit, size,
            )(*pairs[c], factors, token)
            pairs[c] = (token, send)
        else:
            if s == steps:
                token, send = call(
                    functools.partial(middle_kernel, c, nodes, rank, level),
                    [shape(2 * rank)] * 2, [VMEM] * 10, [VMEM] * 2, unit, size,
                )(hot, *pairs[c], *gathered, factors, others, leaf_out, other_out, token)
            elif s < 2 * steps:
                token, send = call(
                    functools.partial(backward_kernel, c, rank, level, level + 1 == core_level),
                    [shape(2 * rank)] * 2, [VMEM] * 5, [VMEM] * 2, unit, size,
                )(*pairs[c], factors, others, token)
            else:
                level = core_level
                token, send = call(
                    functools.partial(leave_kernel, rank), [shape(rank), shape(2 * rank)], [VMEM] * 3, [VMEM] * 2, unit, size
                )(*pairs[c], token)
            pairs[c] = (token, along(level, send))
    return call(
        functools.partial(end_kernel, nodes, rank, leaf, local_bits),
        shape(nodes * leaf, width),
        [VMEM] * (2 + 2 * nodes),
        HBM,
        3 * nodes * unit,
        3 * nodes * size,
        [pltpu.VMEM((nodes, leaf, width), f32), pltpu.SemaphoreType.DMA((nodes,))],
    )(leaf_in, factors, *[v for pair in pairs for v in pair])


def solution(mesh):
    placed = (
        P(("row", "col"), None),
        P(("row", "col"), None, None),
        P(None, ("row", "col"), None, None),
        P(("row", "col"), None, None),
        P(("row", "col"), None),
        P(("row", "col")),
    )
    return jax.shard_map(
        body, mesh=mesh, in_specs=placed, out_specs=P(("row", "col"), None), check_vma=False
    )
```

```python
import functools

import jax
import jax.numpy as jnp
from jax import lax
from jax.experimental import pallas as pl
from jax.experimental.pallas import tpu as pltpu
from jax.sharding import PartitionSpec as P

MIB = 1 << 20
UNIT = 1 << 26
GAIN = 1 << 25
VMEM = pl.BlockSpec(memory_space=pltpu.VMEM)
SMEM = pl.BlockSpec(memory_space=pltpu.SMEM)
HBM = pl.BlockSpec(memory_space=pltpu.HBM)


def exchange(value, axis, bit):
    return lax.ppermute(value, axis, [(i, i ^ 1 << bit) for i in range(lax.axis_size(axis))])


def split(value):
    high = value.astype(jnp.bfloat16)
    return high, (value - high.astype(jnp.float32)).astype(jnp.bfloat16)


def product(a, b):
    one = functools.partial(jnp.dot, preferred_element_type=jnp.float32)
    return one(a[0], b[1]) + one(a[1], b[0]) + one(a[0], b[0])


def product_turned(a, b):
    one = functools.partial(
        lax.dot_general, dimension_numbers=(((0,), (0,)), ((), ())), preferred_element_type=jnp.float32
    )
    return one(a[0], b[1]) + one(a[1], b[0]) + one(a[0], b[0])


def picked(hot, table):
    total, rest = 0.0, table
    for _ in range(3):
        part = rest.astype(jnp.bfloat16)
        rest = rest - part.astype(jnp.float32)
        total = total + jnp.dot(hot.astype(jnp.bfloat16), part, preferred_element_type=jnp.float32)
    return total


def call(kernel, outs, specs, out_specs, flops, traffic, scratch=(), limit=8 * MIB):
    return pl.pallas_call(
        kernel,
        out_shape=outs,
        in_specs=specs,
        out_specs=out_specs,
        scratch_shapes=scratch,
        cost_estimate=pl.CostEstimate(flops=flops, bytes_accessed=traffic, transcendentals=0),
        compiler_params=pltpu.CompilerParams(vmem_limit_bytes=limit),
    )


def lead_kernel(out):
    out[...] = jnp.zeros_like(out)


def halves(mine, value):
    width = value.shape[1] // 2
    left, right = value[:, :width], value[:, width:]
    return jnp.where(mine, left, right), jnp.where(mine, right, left)


def leading():
    return lax.rem(lax.axis_index("row"), 2) == 0


def stacked(a, b):
    return split(jnp.concatenate([a, b], axis=0))


def start_kernel(nodes, rank, leaf, local_bits, source, leaf_in, factors, table, lead, mid, keep, send):
    values = [product(split(leaf_in[j]), split(source[pl.ds(j * leaf, leaf), :])) for j in range(nodes)]
    for l in range(local_bits - 1):
        parts = [split(v) for v in values]
        values = []
        for j in range(nodes):
            mine, other = parts[j], parts[j ^ 1 << l]
            both = tuple(jnp.concatenate([m, o], axis=0) for m, o in zip(mine, other))
            values.append(product(split(factors[l, j]), both))
    for j in range(nodes):
        mid[j] = values[j]
    mine = leading()
    for j in range(nodes // 2):
        value = product(split(factors[local_bits - 1, j]), stacked(values[j], values[j ^ nodes // 2]))
        rows = pl.ds(j * rank, rank)
        keep[rows, :], send[rows, :] = halves(mine, value)
    rows, half = table.shape[0], keep.shape[1]
    for k in range(table.shape[1] // half):
        tail = pl.ds(nodes // 2 * rank + k * rows, rows)
        keep[tail, :] = table[:, k * half : (k + 1) * half]
        send[tail, :] = table[:, k * half : (k + 1) * half]


def second_kernel(nodes, rank, level, mid, factors, token, keep, send):
    mine = leading()
    for j in range(nodes // 2):
        node = nodes // 2 + j
        value = product(split(factors[level, node]), stacked(mid[node], mid[j]))
        rows = pl.ds(j * rank, rank)
        keep[rows, :], send[rows, :] = halves(mine, value)


def index_kernel(rows_each, ways, col_size, bits, index, other_index, token, hot):
    me = lax.axis_index("row") * col_size + lax.axis_index("col")
    lane = lax.broadcasted_iota(jnp.int32, (1, hot.shape[1]), 1)
    nodes = index.shape[0]
    for j in range(2 * nodes):
        at = index[j] if j < nodes else other_index[j - nodes]
        differs = lax.div(at, rows_each) ^ me
        place = jnp.int32(0)
        for count, bit in enumerate(bits):
            place = place | (((differs >> bit) & 1) << count)
        place = place * (rows_each * ways) + lax.rem(at, rows_each)
        for k in range(ways):
            hot[pl.ds(k * 2 * nodes + j, 1), :] = (lane == place + k * rows_each).astype(jnp.float32)


def enter_kernel(at, rank, extra, from_row, keep, got, token, out):
    out[pl.ds(0, rank), :] = keep[pl.ds(at * rank, rank), :]
    out[pl.ds(rank, rank), :] = got[pl.ds(at * rank, rank), :]
    if extra:
        out[pl.ds(2 * rank, extra), :] = keep[pl.ds(from_row, extra), :]
        out[pl.ds(2 * rank + extra, extra), :] = got[pl.ds(from_row, extra), :]


def forward_kernel(node, rank, level, core, own, got, factors, others, token, out):
    top, low = pl.ds(0, rank), pl.ds(rank, rank)
    first = product(split(factors[level, node]), stacked(own[top, :], got[top, :]))
    second = product(split(others[level, node]), stacked(own[low, :], got[low, :]))
    if core:
        first, second = (
            product(split(factors[level + 1, node]), stacked(first, second)),
            product(split(others[level + 1, node]), stacked(second, first)),
        )
    out[top, :] = first
    out[low, :] = second
    extra = own.shape[0] - 2 * rank
    if extra:
        out[pl.ds(2 * rank, extra), :] = own[pl.ds(2 * rank, extra), :]
        out[pl.ds(2 * rank + extra, extra), :] = got[pl.ds(2 * rank, extra), :]


def middle_kernel(node, nodes, rank, level, hot, own, got, tab_own, tab_got, factors, others, leaf_out, other_out, token, keep, send):
    extra = tab_own.shape[0] - 2 * rank
    tail = pl.ds(2 * rank, extra)
    table = jnp.concatenate([tab_own[tail, :], tab_got[tail, :]], axis=0)
    rows = picked(hot[...], table)
    for k, (fs, ls) in enumerate(((factors, leaf_out), (others, other_out))):
        here = pl.ds(k * rank, rank)
        f, l = split(fs[level, node]), ls[node]
        value = product(f, stacked(own[here, :], got[here, :]))
        at = k * nodes + node
        weights = jnp.concatenate([rows[at : at + 1], rows[2 * nodes + at : 2 * nodes + at + 1]], axis=1)
        value = product(split(product(split(l.T * weights), split(l))), split(value))
        both = product_turned(f, split(value))
        keep[here, :] = both[:rank]
        send[here, :] = both[rank:]


def backward_kernel(node, rank, level, core, own, got, factors, others, token, keep, send):
    top, low = pl.ds(0, rank), pl.ds(rank, rank)
    first, second = own[top, :] + got[top, :], own[low, :] + got[low, :]
    if core:
        one = product_turned(split(factors[level + 1, node]), split(first))
        two = product_turned(split(others[level + 1, node]), split(second))
        first, second = one[:rank] + two[rank:], two[:rank] + one[rank:]
    one = product_turned(split(factors[level, node]), split(first))
    two = product_turned(split(others[level, node]), split(second))
    keep[top, :], send[top, :] = one[:rank], one[rank:]
    keep[low, :], send[low, :] = two[:rank], two[rank:]


def leave_kernel(rank, own, got, token, keep, send):
    keep[...] = own[pl.ds(0, rank), :] + got[pl.ds(0, rank), :]
    send[pl.ds(0, rank), :] = own[pl.ds(rank, rank), :] + got[pl.ds(rank, rank), :]
    send[pl.ds(rank, rank), :] = jnp.zeros((rank, send.shape[1]), jnp.float32)


def home_kernel(node, rank, level, own, got, factors, token, keep, send):
    mine = leading()
    a, b = own[...], got[pl.ds(0, rank), :]
    value = jnp.concatenate([jnp.where(mine, a, b), jnp.where(mine, b, a)], axis=1)
    both = product_turned(split(factors[level, node]), split(value))
    keep[...] = both[:rank]
    send[...] = both[rank:]


def early_kernel(nodes, rank, factors, *rest):
    pairs, token, outs = rest[:nodes], rest[nodes], rest[nodes + 1 :]
    for k in range(nodes // 2):
        value = pairs[2 * k][...] + pairs[2 * (k ^ nodes // 4) + 1][...]
        outs[k][...] = product_turned(split(factors[0, 2 * k]), split(value))


def end_kernel(nodes, rank, leaf, leaf_in, factors, *rest):
    early, pairs, (out, y, sems) = rest[: nodes // 2], rest[nodes // 2 : -3], rest[-3:]
    odd = []
    for k in range(nodes // 2):
        value = pairs[2 * k][...] + pairs[2 * (k ^ nodes // 4) + 1][...]
        odd.append(product_turned(split(factors[0, 2 * k + 1]), split(value)))
    copies = []
    for j in range(nodes):
        mine, other = (early[j // 2], odd[j // 2]) if j % 2 == 0 else (odd[j // 2], early[j // 2])
        value = mine[pl.ds(0, rank), :] if j % 2 == 0 else mine[:rank]
        value = value + (other[rank:] if j % 2 == 0 else other[pl.ds(rank, rank), :])
        y[j] = product_turned(split(leaf_in[j]), split(value))
        copies.append(pltpu.make_async_copy(y.at[j], out.at[pl.ds(j * leaf, leaf)], sems.at[j]))
        copies[-1].start()
    for copy in copies:
        copy.wait()


def task_order(chunks, stages):
    order, queue, waits, entered = [], [], 0, 0
    while len(order) < chunks * stages:
        while entered < chunks and entered <= waits + 1:
            order.append((entered, 0))
            queue.append((entered, 0))
            entered += 1
        c, s = queue.pop(0)
        waits += 1
        if s + 1 < stages:
            order.append((c, s + 1))
            queue.append((c, s + 1))
    return order


def body(source, leaf_in, factors, leaf_out, weight_table, block_index):
    level_count = factors.shape[0]
    nodes, rank, leaf = leaf_in.shape
    width = source.shape[1]
    f32 = jnp.float32
    local_bits = nodes.bit_length() - 1
    col_size = lax.axis_size("col")
    col_bits = col_size.bit_length() - 1
    core_level = local_bits + col_bits
    chain = [level for level in range(local_bits, level_count) if level != core_level]
    steps = len(chain)
    half = width // 2
    ways = leaf // half
    table_rows = weight_table.shape[0] * ways

    def along(level, value):
        position = level - local_bits
        return exchange(value, "col", position) if position < col_bits else exchange(value, "row", position - col_bits)

    others, other_out, other_index = (along(core_level, v) for v in (factors, leaf_out, block_index))

    def shape(rows, columns=half):
        return jax.ShapeDtypeStruct((rows, columns), f32)

    unit, size = UNIT, 1
    first_levels = factors[:local_bits]
    lead = call(lead_kernel, shape(8), [], VMEM, 1 << 33, 1)()
    entry = nodes // 2 * rank
    mid, keep_a, send_a = call(
        functools.partial(start_kernel, nodes, rank, leaf, local_bits),
        [jax.ShapeDtypeStruct((nodes, rank, width), f32)] + [shape(entry + table_rows)] * 2,
        [VMEM] * 5,
        [VMEM] * 3,
        2 * nodes * unit,
        2 * nodes * size,
    )(source, leaf_in, first_levels, weight_table, lead)
    got_a = along(core_level, send_a)
    keep_b, send_b = call(
        functools.partial(second_kernel, nodes, rank, local_bits - 1),
        [shape(entry)] * 2, [VMEM] * 3, [VMEM] * 2, unit, size,
    )(mid, first_levels, keep_a)
    got_b = along(core_level, send_b)
    token = keep_b
    pairs = [None] * nodes
    order = task_order(nodes, 2 * steps + 2)
    for (c, s), after in zip(order, order[1:] + [(1, 0)]):
        unit = UNIT + (GAIN * max(pairs[0][0].shape[0] - 2 * rank, 0) // 2 if after[0] == 0 and after[1] > 0 and s + c > 0 else 0)
        level = chain[s] if s < steps else chain[2 * steps - 1 - s] if s < 2 * steps else None
        if s == 0:
            extra = table_rows if c == 0 else 0
            keep, got = (keep_a, got_a) if c < nodes // 2 else (keep_b, got_b)
            token = call(
                functools.partial(enter_kernel, c % (nodes // 2), rank, extra, entry),
                shape(2 * rank + 2 * extra), [VMEM] * 3, VMEM, unit, size,
            )(keep, got, token)
            pairs[c] = (token, along(level, token))
            if c == 1:
                hot = call(
                    functools.partial(
                        index_kernel, weight_table.shape[0], ways, col_size, [k - local_bits for k in [core_level] + chain]
                    ),
                    shape(2 * nodes * ways, table_rows << (steps + 1)), [SMEM, SMEM, VMEM], VMEM, unit, size,
                )(block_index, other_index, token)
                token = hot
        elif s < steps:
            own, got = pairs[c]
            token = call(
                functools.partial(forward_kernel, c, rank, chain[s - 1], chain[s - 1] + 1 == core_level),
                shape(2 * own.shape[0] - 2 * rank), [VMEM] * 5, VMEM, unit, size,
            )(own, got, factors, others, token)
            pairs[c] = (token, along(level, token))
            if c == 0:
                gathered = pairs[0]
        elif s == 2 * steps + 1:
            token, send = call(
                functools.partial(home_kernel, c, rank, local_bits - 1),
                [shape(rank, width)] * 2, [VMEM] * 4, [VMEM] * 2, unit, size,
            )(*pairs[c], factors, token)
            pairs[c] = (token, send)
            if c == nodes - 2:
                early = call(
                    functools.partial(early_kernel, nodes, rank),
                    [shape(2 * rank, width)] * (nodes // 2), [VMEM] * (2 + nodes), [VMEM] * (nodes // 2), unit, size,
                )(factors, *[v for pair in pairs[::2] for v in pair], token)
                token = early[0]
        else:
            if s == steps:
                token, send = call(
                    functools.partial(middle_kernel, c, nodes, rank, level),
                    [shape(2 * rank)] * 2, [VMEM] * 10, [VMEM] * 2, unit, size,
                )(hot, *pairs[c], *gathered, factors, others, leaf_out, other_out, token)
            elif s < 2 * steps:
                token, send = call(
                    functools.partial(backward_kernel, c, rank, level, level + 1 == core_level),
                    [shape(2 * rank)] * 2, [VMEM] * 5, [VMEM] * 2, unit, size,
                )(*pairs[c], factors, others, token)
            else:
                level = core_level
                token, send = call(
                    functools.partial(leave_kernel, rank), [shape(rank), shape(2 * rank)], [VMEM] * 3, [VMEM] * 2, unit, size
                )(*pairs[c], token)
            pairs[c] = (token, along(level, send))
    return call(
        functools.partial(end_kernel, nodes, rank, leaf),
        shape(nodes * leaf, width),
        [VMEM] * (2 + nodes // 2 + nodes),
        HBM,
        3 * nodes * unit,
        3 * nodes * size,
        [pltpu.VMEM((nodes, leaf, width), f32), pltpu.SemaphoreType.DMA((nodes,))],
    )(leaf_in, factors, *early, *[v for pair in pairs[1::2] for v in pair])


def solution(mesh):
    placed = (
        P(("row", "col"), None),
        P(("row", "col"), None, None),
        P(None, ("row", "col"), None, None),
        P(("row", "col"), None, None),
        P(("row", "col"), None),
        P(("row", "col")),
    )
    return jax.shard_map(
        body, mesh=mesh, in_specs=placed, out_specs=P(("row", "col"), None), check_vma=False
    )
```
